256 devices in a mesh: dp: 64 (over z, x, core), tensor: 4 (over y).
Axes of the slice: x: 4, y: 4, z: 8, core: 2. Of those that a mesh axis runs over, the one named last changes fastest.
Arguments:
- grad_blocks: float32 [128, 512, 512], P('tensor', 'dp'), may hold values from -420 to 420
- owner_map: int32 [4, 32], replicated, may hold values from 0 to 63, as said below
- left_state: float32 [4, 64, 2, 512, 512], P('tensor', 'dp'), may hold values from -1 to 5, as said below
- right_state: float32 [4, 64, 2, 512, 512], P('tensor', 'dp'), may hold values from -1 to 5, as said below
Outputs:
- step_blocks: float32 [128, 512, 512], P('tensor', 'dp')
- new_left: float32 [4, 64, 2, 512, 512], P('tensor', 'dp')
- new_right: float32 [4, 64, 2, 512, 512], P('tensor', 'dp')
The draws below stay inside these ranges and needn't reach their ends.
Inputs may be any that keep to these rules, and one draw needn't show every extreme that they name: `owner_map`: within one tensor index every dp index owns at most 2 blocks, and one owns exactly 2. `left_state`: every block is symmetric positive definite. `right_state`: every block is symmetric positive definite.
All inputs are finite; a program needn't handle non-finite values.
Results may differ from the reference program's by a relative error of at most 0.013.
Values sent between devices are 32-bit elements; how exact they have to be, the bound alone decides.
A program may use at most 64 MiB of HBM per device.

```python
import math
import jax
import jax.numpy as jnp
from jax import lax

B = 512
ITERS = 2
NBLK = 32
MOST = 2
TBLK = 128
N_DP = 64
N_TENSOR = 4


def draw_grad_blocks(key, part):
    key = jax.random.fold_in(key, 11)
    noise_key = jax.random.fold_in(key, 0)
    row_key = jax.random.fold_in(key, 2)
    column_key = jax.random.fold_in(key, 3)
    full_shape = (TBLK, B, B)
    row_place = jnp.arange(B, dtype=jnp.float32) / (B - 1)
    block_place = jnp.arange(TBLK, dtype=jnp.float32) / max(TBLK - 1, 1)
    rising = jnp.exp(0.5 * math.log(3.0) * row_place)[None, :, None] * jnp.exp(0.5 * math.log(3.0) * block_place)[:, None, None]
    base = jnp.clip(jax.random.normal(noise_key, full_shape, jnp.float32), -6.0, 6.0)
    row_scale = jnp.exp(jax.random.uniform(row_key, (TBLK, B, 1), jnp.float32, math.log(0.5), math.log(5.0)))
    column_scale = jnp.exp(jax.random.uniform(column_key, (TBLK, 1, B), jnp.float32, math.log(0.4), math.log(4.0)))
    return base * row_scale * column_scale * rising


def draw_owner_map(key, part):
    key = jax.random.fold_in(key, 5)
    row_keys = jax.random.split(key, N_TENSOR)

    def one_row(row_key):
        pick_key, spread_key, shuffle_key = jax.random.split(row_key, 3)
        capacity = N_DP * MOST
        busiest = jax.random.randint(pick_key, (), 0, N_DP)
        others = jax.random.permutation(spread_key, capacity - MOST)
        picked = (busiest * MOST + MOST + others) % capacity
        slot_list = jnp.concatenate([busiest * MOST + jnp.arange(MOST), picked])[:NBLK]
        order_perm = jax.random.permutation(shuffle_key, NBLK)
        return (slot_list[order_perm] // MOST).astype(jnp.int32)
    return jax.vmap(one_row)(row_keys)


def factor_blocks(key, diag_lo, diag_hi, spread):
    diag_key, off_key = jax.random.split(key)
    lead = (N_TENSOR, N_DP, MOST)
    diagonal = jnp.exp(jax.random.uniform(diag_key, lead + (B,), jnp.float32, math.log(diag_lo), math.log(diag_hi)))
    uneven = jax.random.uniform(off_key, lead + (B, B), jnp.float32, -spread, spread) / B
    symmetric = 0.5 * (uneven + jnp.swapaxes(uneven, -1, -2))
    return symmetric + diagonal[..., :, None] * jnp.eye(B, dtype=jnp.float32)


def draw_left_state(key, part):
    key = jax.random.fold_in(key, 12)
    return factor_blocks(key, 0.5, 2.0, 0.4)


def draw_right_state(key, part):
    key = jax.random.fold_in(key, 13)
    return factor_blocks(key, 0.5, 2.0, 0.4)


def setup_inputs(seed: int = 0) -> dict:
    seeds = jax.random.split(jax.random.key(seed), 5)
    grad_blocks = draw_grad_blocks(jax.random.fold_in(seeds[4], 71), 0)
    owner_map = draw_owner_map(jax.random.fold_in(seeds[4], 71), 0)
    left_state = draw_left_state(jax.random.fold_in(seeds[4], 71), 0)
    right_state = draw_right_state(jax.random.fold_in(seeds[4], 71), 0)
    return {"grad_blocks": grad_blocks, "owner_map": owner_map, "left_state": left_state, "right_state": right_state}


def rounded(value):
    return lax.optimization_barrier(value.astype(jnp.bfloat16)).astype(jnp.float32)

def product(left_op, right_op):
    return jnp.dot(rounded(left_op), rounded(right_op), precision=lax.Precision.HIGHEST)

def inverse_root(factor):
    identity = jnp.eye(factor.shape[0], dtype=jnp.float32)
    scaling = 2.5 / jnp.sqrt(jnp.sum(factor * factor) + 1e-06)
    root_est = jnp.sqrt(jnp.sqrt(scaling)) * identity
    matrix = scaling * factor
    for sweep in range(ITERS):
        stepper = 1.25 * identity - 0.25 * matrix
        root_est = product(root_est, stepper)
        square = product(stepper, stepper)
        fourth = product(square, square)
        matrix = product(fourth, matrix)
    return root_est

def update_block(clipped, left_old, right_old):
    block_order = clipped.shape[0]
    gram_left = lax.dot_general(clipped, clipped, (((1,), (1,)), ((), ())), precision=lax.Precision.HIGHEST)
    gram_right = lax.dot_general(clipped, clipped, (((0,), (0,)), ((), ())), precision=lax.Precision.HIGHEST)
    left_new = 0.9 * left_old + 0.1 * gram_left / block_order
    right_new = 0.9 * right_old + 0.1 * gram_right / block_order
    left_root = inverse_root(left_new)
    right_root = inverse_root(right_new)
    middle = product(left_root, clipped)
    direction = product(middle, right_root)
    graft_ratio = jnp.sqrt(jnp.sum(clipped * clipped) + 1e-06) / jnp.sqrt(jnp.sum(direction * direction) + 1e-06)
    return (-graft_ratio * direction, left_new, right_new)

def reference(grad_blocks, owner_map, left_state, right_state):
    block_total = grad_blocks.shape[0]
    block_order = grad_blocks.shape[1]
    squares = jnp.sum(grad_blocks * grad_blocks)
    clip_factor = 1.0 / jnp.sqrt(squares / (block_total * block_order * block_order) + 1e-06)
    positions = jnp.arange(NBLK)
    same_owner = owner_map[:, :, None] == owner_map[:, None, :]
    earlier = positions[:, None] < positions[None, :]
    slot_of = lax.optimization_barrier(jnp.sum(jnp.where(same_owner & earlier[None], 1, 0), axis=1)).astype(jnp.int32).reshape(-1)
    tensor_of = (jnp.arange(block_total) // NBLK).astype(jnp.int32)
    owner_of = owner_map.reshape(-1).astype(jnp.int32)
    left_old = left_state[tensor_of, owner_of, slot_of]
    right_old = right_state[tensor_of, owner_of, slot_of]

    def one_block(items):
        return update_block(clip_factor * items[0], items[1], items[2])
    step_blocks, left_new, right_new = lax.map(one_block, (grad_blocks, left_old, right_old))
    new_left = jnp.zeros_like(left_state).at[tensor_of, owner_of, slot_of].set(left_new)
    new_right = jnp.zeros_like(right_state).at[tensor_of, owner_of, slot_of].set(right_new)
    return (step_blocks, new_left, new_right)
```

```python
import functools

import jax
import jax.numpy as jnp
from jax import lax
from jax.experimental import pallas as pl
from jax.experimental.pallas import tpu as pltpu
from jax.sharding import PartitionSpec as P

MESH = pl.DeviceIdType.MESH
F32 = jnp.float32
BF16 = jnp.bfloat16


def matmul(a, b):
    return jnp.dot(a, b, preferred_element_type=F32)


def total(x):
    return jnp.sum(x, keepdims=True)


def scaled_root(factor, eye):
    scaling = 2.5 * lax.rsqrt(total(factor * factor) + 1e-06)
    matrix = scaling * factor
    step_one = jnp.where(eye, 1.25, 0.0) - 0.25 * matrix
    step_one = step_one.astype(BF16)
    square = matmul(step_one, step_one).astype(BF16)
    fourth = matmul(square, square).astype(BF16)
    matrix = matmul(fourth, matrix.astype(BF16))
    step_two = (jnp.where(eye, 1.25, 0.0) - 0.25 * matrix).astype(BF16)
    return matmul(step_one, step_two), scaling


def kernel(
    n_dp, n_tensor, blocks,
    source_ref, place_ref, filled_ref, grad_ref, left_ref, right_ref,
    step_ref, new_left_ref, new_right_ref,
    packed, arrived, left, right, steps, returned, sums_y, sums_p, sums_z, mine_y, mine_p, mine_z,
    state_sem, out_sem, send_sem, recv_sem, back_send, back_recv, sum_send, sum_recv,
):
    me = lax.axis_index("dp")
    tensor = lax.axis_index("tensor")
    slots = arrived.shape[0]
    plane = 8
    depth = n_dp // plane
    my_z = me // plane
    my_p = lax.rem(me, plane)
    order = arrived.shape[1] * arrived.shape[2]

    for slot in range(slots):
        pltpu.make_async_copy(left_ref.at[slot], left.at[slot], state_sem.at[0, slot]).start()
        pltpu.make_async_copy(right_ref.at[slot], right.at[slot], state_sem.at[1, slot]).start()

    barrier = pltpu.get_barrier_semaphore()

    def greet(i, _):
        pl.semaphore_signal(barrier, inc=1, device_id=(lax.rem(me + i, n_dp), tensor), device_id_type=MESH)
        return 0

    lax.fori_loop(1, n_dp, greet, 0)
    for i in range(1, n_tensor):
        pl.semaphore_signal(barrier, inc=1, device_id=(me, lax.rem(tensor + i, n_tensor)), device_id_type=MESH)

    grads = grad_ref[...]
    squares = jnp.sum(grads * grads, axis=0)
    tile = squares[:, :128]
    for i in range(1, squares.shape[1] // 128):
        tile = tile + squares[:, i * 128:(i + 1) * 128]
    mine_y[...] = tile
    sums_y[tensor] = tile

    def pack(q, _):
        for slot in range(slots):
            packed[slot, q] = grad_ref[source_ref[slot * n_dp + q]]
        return 0

    lax.fori_loop(0, n_dp, pack, 0)
    pl.semaphore_wait(barrier, n_dp - 1 + n_tensor - 1)

    def peer(i):
        z = lax.rem(my_z + lax.rem(i, depth), depth)
        p = lax.rem(my_p + i // depth, plane)
        return z * plane + p

    def tell(src, dst, stage, device):
        pltpu.make_async_remote_copy(
            src_ref=src, dst_ref=dst, send_sem=sum_send.at[stage], recv_sem=sum_recv.at[stage],
            device_id=device, device_id_type=MESH,
        ).start()

    def heard(sums, stage, count):
        others = sums.at[pl.ds(0, count)]
        pltpu.make_async_copy(others, others, sum_recv.at[stage]).wait()
        pltpu.make_async_copy(others, others, sum_send.at[stage]).wait()

    def send_slot(slot):
        def go(i, _):
            to = peer(i)
            pltpu.make_async_remote_copy(
                src_ref=packed.at[slot, to], dst_ref=arrived.at[slot, me],
                send_sem=send_sem.at[slot], recv_sem=recv_sem.at[slot],
                device_id=(to, tensor), device_id_type=MESH,
            ).start()
            return 0

        lax.fori_loop(1, n_dp, go, 0)
        pltpu.make_async_copy(packed.at[slot, me], arrived.at[slot, me], recv_sem.at[slot]).start()

    for i in range(1, n_tensor):
        tell(mine_y, sums_y.at[tensor], 0, (me, lax.rem(tensor + i, n_tensor)))
    send_slot(0)
    heard(sums_y, 0, n_tensor - 1)
    tile = jnp.sum(sums_y[...], axis=0)
    mine_p[...] = tile
    sums_p[my_p] = tile
    for i in range(1, plane):
        tell(mine_p, sums_p.at[my_p], 1, (my_z * plane + lax.rem(my_p + i, plane), tensor))
    for slot in range(1, slots):
        send_slot(slot)
    heard(sums_p, 1, plane - 1)
    tile = jnp.sum(sums_p[...], axis=0)
    mine_z[...] = tile
    sums_z[my_z] = tile
    for i in range(1, depth):
        tell(mine_z, sums_z.at[my_z], 2, (lax.rem(my_z + i, depth) * plane + my_p, tensor))
    heard(sums_z, 2, depth - 1)
    entries = blocks * n_tensor * order * order
    clip = lax.rsqrt(total(jnp.sum(sums_z[...], axis=0)) / entries + 1e-06)
    clip_sq = clip * clip

    eye = lax.broadcasted_iota(jnp.int32, (order, order), 0) == lax.broadcasted_iota(jnp.int32, (order, order), 1)

    def update(slot, _):
        filled = filled_ref[slot]
        pltpu.make_async_copy(arrived.at[slot], arrived.at[slot], recv_sem.at[slot]).wait()
        pltpu.make_async_copy(left.at[slot], left.at[slot], state_sem.at[0, slot]).wait()
        pltpu.make_async_copy(right.at[slot], right.at[slot], state_sem.at[1, slot]).wait()
        grad = arrived[slot].reshape(order, order)
        grad_sq = total(grad * grad)
        grad = grad.astype(BF16)
        gram = clip_sq * (0.1 / order)
        left_new = 0.9 * left[slot] + gram * lax.dot_general(
            grad, grad, (((1,), (1,)), ((), ())), preferred_element_type=F32)
        left[slot] = filled * left_new
        right_new = 0.9 * right[slot] + gram * lax.dot_general(
            grad, grad, (((0,), (0,)), ((), ())), preferred_element_type=F32)
        right[slot] = filled * right_new
        pltpu.make_async_copy(left.at[slot], new_left_ref.at[slot], out_sem.at[0, slot]).start()
        pltpu.make_async_copy(right.at[slot], new_right_ref.at[slot], out_sem.at[1, slot]).start()
        left_root, left_scale = scaled_root(left_new, eye)
        right_root, right_scale = scaled_root(right_new, eye)
        middle = matmul(left_root.astype(BF16), grad).astype(BF16)
        direction = matmul(middle, right_root.astype(BF16))
        scale = clip * jnp.sqrt(jnp.sqrt(left_scale * right_scale))
        ratio = jnp.sqrt(clip_sq * grad_sq + 1e-06) * lax.rsqrt(scale * scale * total(direction * direction) + 1e-06)
        steps[slot] = ((-ratio * scale) * direction).reshape(n_dp, order // n_dp, order)

        def back(i, _):
            to = peer(i)
            pltpu.make_async_remote_copy(
                src_ref=steps.at[slot, to], dst_ref=returned.at[slot, me],
                send_sem=back_send.at[slot], recv_sem=back_recv.at[slot],
                device_id=(to, tensor), device_id_type=MESH,
            ).start()
            return 0

        lax.fori_loop(1, n_dp, back, 0)
        pltpu.make_async_copy(steps.at[slot, me], returned.at[slot, me], back_recv.at[slot]).start()
        return 0

    lax.fori_loop(0, slots, update, 0)

    for slot in range(slots):
        others = packed.at[slot, pl.ds(0, n_dp - 1)]
        pltpu.make_async_copy(others, others, send_sem.at[slot]).wait()
        pltpu.make_async_copy(left.at[slot], new_left_ref.at[slot], out_sem.at[0, slot]).wait()
        pltpu.make_async_copy(right.at[slot], new_right_ref.at[slot], out_sem.at[1, slot]).wait()
    for slot in range(slots):
        pltpu.make_async_copy(returned.at[slot], returned.at[slot], back_recv.at[slot]).wait()
        others = steps.at[slot, pl.ds(0, n_dp - 1)]
        pltpu.make_async_copy(others, others, back_send.at[slot]).wait()

    def pick(j, _):
        step_ref[j] = returned[place_ref[blocks + j], place_ref[j]]
        return 0

    lax.fori_loop(0, blocks, pick, 0)


def local(grad_blocks, owner_map, left_state, right_state):
    blocks, rows, order = grad_blocks.shape
    slots = left_state.shape[2]
    n_dp = lax.axis_size("dp")
    n_tensor = lax.axis_size("tensor")
    owners = lax.dynamic_slice_in_dim(owner_map, lax.axis_index("tensor"), 1, 0)[0]
    positions = jnp.arange(blocks, dtype=jnp.int32)
    same_owner = owners[:, None] == owners[None, :]
    earlier = positions[:, None] < positions[None, :]
    slot_of = jnp.sum(jnp.where(same_owner & earlier, 1, 0), axis=0).astype(jnp.int32)
    target = slot_of * n_dp + owners
    hit = jnp.arange(slots * n_dp, dtype=jnp.int32)[None, :] == target[:, None]
    source = jnp.sum(jnp.where(hit, positions[:, None], 0), axis=0).astype(jnp.int32)
    place = jnp.concatenate([owners, slot_of])
    owned = jnp.sum(jnp.where(owners == lax.axis_index("dp"), 1, 0))
    filled = (jnp.arange(slots) < owned).astype(F32)

    smem = pl.BlockSpec(memory_space=pltpu.SMEM)
    vmem = pl.BlockSpec(memory_space=pltpu.VMEM)
    hbm = pl.BlockSpec(memory_space=pl.ANY)
    step_blocks, new_left, new_right = pl.pallas_call(
        functools.partial(kernel, n_dp, n_tensor, blocks),
        out_shape=(
            jax.ShapeDtypeStruct((blocks, rows, order), F32),
            jax.ShapeDtypeStruct((slots, order, order), F32),
            jax.ShapeDtypeStruct((slots, order, order), F32),
        ),
        in_specs=[smem, smem, smem, vmem, hbm, hbm],
        out_specs=(vmem, hbm, hbm),
        scratch_shapes=[
            pltpu.VMEM((slots, n_dp, rows, order), F32),
            pltpu.VMEM((slots, n_dp, rows, order), F32),
            pltpu.VMEM((slots, order, order), F32),
            pltpu.VMEM((slots, order, order), F32),
            pltpu.VMEM((slots, n_dp, rows, order), F32),
            pltpu.VMEM((slots, n_dp, rows, order), F32),
            pltpu.VMEM((n_tensor, 8, 128), F32),
            pltpu.VMEM((8, 8, 128), F32),
            pltpu.VMEM((n_dp // 8, 8, 128), F32),
            pltpu.VMEM((8, 128), F32),
            pltpu.VMEM((8, 128), F32),
            pltpu.VMEM((8, 128), F32),
            pltpu.SemaphoreType.DMA((2, slots)),
            pltpu.SemaphoreType.DMA((2, slots)),
            pltpu.SemaphoreType.DMA((slots,)),
            pltpu.SemaphoreType.DMA((slots,)),
            pltpu.SemaphoreType.DMA((slots,)),
            pltpu.SemaphoreType.DMA((slots,)),
            pltpu.SemaphoreType.DMA((3,)),
            pltpu.SemaphoreType.DMA((3,)),
        ],
        compiler_params=pltpu.CompilerParams(
            collective_id=0, has_side_effects=True, vmem_limit_bytes=48 * 2**20
        ),
        cost_estimate=pl.CostEstimate(flops=slots * 24 * order**3, bytes_accessed=18 * order * order, transcendentals=0),
    )(source, place, filled, grad_blocks, left_state[0, 0], right_state[0, 0])
    return (step_blocks, new_left[None, None], new_right[None, None])


def solution(mesh):
    state = P("tensor", "dp", None, None, None)
    return jax.shard_map(
        local,
        mesh=mesh,
        in_specs=(P("tensor", "dp", None), P(), state, state),
        out_specs=(P("tensor", "dp", None), state, state),
        check_vma=False,
    )
```

```python
import functools

import jax
import jax.numpy as jnp
from jax import lax
from jax.experimental import pallas as pl
from jax.experimental.pallas import tpu as pltpu
from jax.sharding import PartitionSpec as P

MESH = pl.DeviceIdType.MESH
F32 = jnp.float32
BF16 = jnp.bfloat16
I32 = jnp.int32
PLANE = 8
BUNDLE = 4


def matmul(a, b):
    return jnp.dot(a, b, preferred_element_type=F32)


def total(x):
    return jnp.sum(x, keepdims=True)


def scaled_root(factor, eye):
    scaling = 2.5 * lax.rsqrt(total(factor * factor) + 1e-06)
    matrix = scaling * factor
    step_one = jnp.where(eye, 1.25, 0.0) - 0.25 * matrix
    step_one = step_one.astype(BF16)
    square = matmul(step_one, step_one).astype(BF16)
    fourth = matmul(square, square).astype(BF16)
    matrix = matmul(fourth, matrix.astype(BF16))
    step_two = (jnp.where(eye, 1.25, 0.0) - 0.25 * matrix).astype(BF16)
    return matmul(step_one, step_two), scaling


def plan(owners, me, n_dp, bundled):
    blocks = owners.shape[1]
    sub = lax.broadcasted_iota(I32, (blocks, blocks), 0)
    lane = lax.broadcasted_iota(I32, (blocks, blocks), 1)
    across = jnp.broadcast_to(owners, (blocks, blocks))

    def column(row):
        return jnp.sum(jnp.where(sub == lane, row, 0), axis=1, keepdims=True)

    owner = column(across)
    same = across == owner
    slot = jnp.sum(jnp.where(same & (lane < sub), 1, 0), axis=1, keepdims=True)
    slot_row = jnp.sum(jnp.where(same & (sub < lane), 1, 0), axis=0, keepdims=True)
    depth_of, place_of = owner // PLANE, owner % PLANE
    second_row = jnp.broadcast_to(jnp.where(slot_row == 1, owners, n_dp * 2), (blocks, blocks))
    rank = jnp.sum(jnp.where((second_row // PLANE == depth_of) & (second_row < owner), 1, 0), axis=1, keepdims=True)
    key = jnp.where(slot == 1, depth_of * BUNDLE + rank, -1)
    wide = lax.broadcasted_iota(I32, (blocks, 128), 1)
    block = lax.broadcasted_iota(I32, (blocks, 128), 0)

    def row(value):
        return jnp.sum(value, axis=0, keepdims=True)

    first_of = row(jnp.where((slot == 0) & (owner == wide), block, 0))
    second_of = row(jnp.where((slot == 1) & (owner == wide), block, 0))
    bundle_of = row(jnp.where(key == wide, block, 0))
    rank_of = row(jnp.where((slot == 1) & (owner == wide), rank, 0))
    place_at = row(jnp.where(key == wide, place_of, 0))
    found = jnp.where(slot == 1, n_dp + (key if bundled else owner), owner)
    pick = row(jnp.where(block == wide, found, 0))
    owned = jnp.sum(jnp.where(owners == me, 1, 0), keepdims=True)
    return (first_of, second_of, bundle_of, rank_of, place_at, pick), owned


FIRST, SECOND, BUNDLED, RANK, PLACE, PICK = range(6)


def kernel(
    n_dp, n_tensor, bundled,
    owner_ref, grad_ref, left_ref, right_ref,
    step_ref, new_left_ref, new_right_ref,
    grads, packed, arrived, left, right, steps, returned, z_out, z_in, x_back, z_back,
    sums_z, sums_p, sums_y, mine_z, mine_p, mine_y, rows_v, rows_s,
    local_sem, state_sem, out_sem, send_sem, recv_sem, back_send, back_recv, hop_send, hop_recv, sum_send, sum_recv,
):
    me = lax.axis_index("dp")
    tensor = lax.axis_index("tensor")
    blocks = grads.shape[0]
    slots, depth = arrived.shape[:2]
    rows, order = grads.shape[1:]
    my_z = me // PLANE
    my_p = lax.rem(me, PLANE)

    get_grads = pltpu.make_async_copy(grad_ref, grads, local_sem.at[0])
    get_grads.start()

    barrier = pltpu.get_barrier_semaphore()

    def greet(i, _):
        pl.semaphore_signal(barrier, inc=1, device_id=(lax.rem(me + i, n_dp), tensor), device_id_type=MESH)
        return 0

    lax.fori_loop(1, n_dp, greet, 0)
    for i in range(1, n_tensor):
        pl.semaphore_signal(barrier, inc=1, device_id=(me, lax.rem(tensor + i, n_tensor)), device_id_type=MESH)

    tables, owned = plan(owner_ref[pl.ds(tensor, 1), :], me, n_dp, bundled)
    rows_v[...] = jnp.concatenate(tables + (tables[0], tables[0]), axis=0)
    put_rows = pltpu.make_async_copy(rows_v, rows_s, local_sem.at[1])
    put_rows.start()
    for slot in range(slots):
        pltpu.make_async_copy(left_ref.at[slot], left.at[slot], state_sem.at[0, slot]).start()
        pltpu.make_async_copy(right_ref.at[slot], right.at[slot], state_sem.at[1, slot]).start()

    get_grads.wait()
    tile = jnp.zeros((8, 128), F32)
    for k in range(order // 128):
        part = grads[:, :, k * 128:(k + 1) * 128]
        tile = tile + jnp.sum(part * part, axis=0)
    mine_z[...] = tile
    sums_z[my_z] = tile
    put_rows.wait()

    if bundled:
        def pack_bundle(q, _):
            z_out[q] = grads[rows_s[BUNDLED, q]]
            return 0

        lax.fori_loop(0, depth * BUNDLE, pack_bundle, 0)

    def pack(q, _):
        z, p = q // PLANE, lax.rem(q, PLANE)
        packed[0, z, p] = grads[rows_s[FIRST, q]]
        if not bundled:
            packed[1, z, p] = grads[rows_s[SECOND, q]]
        return 0

    lax.fori_loop(0, n_dp, pack, 0)
    pl.semaphore_wait(barrier, n_dp - 1 + n_tensor - 1)

    def copy(src, dst, send, recv, to):
        pltpu.make_async_remote_copy(
            src_ref=src, dst_ref=dst, send_sem=send, recv_sem=recv, device_id=to, device_id_type=MESH
        ).start()

    def wait(ref, sem):
        pltpu.make_async_copy(ref, ref, sem).wait()

    def peer(i):
        return lax.rem(my_z + lax.rem(i, depth), depth), lax.rem(my_p + i // depth, PLANE)

    def along_z(i):
        return lax.rem(my_z + i, depth)

    def in_plane(i):
        return lax.rem(my_p + i, PLANE)

    def heard(sums, stage, count):
        wait(sums.at[pl.ds(0, count)], sum_recv.at[stage])
        wait(sums.at[pl.ds(0, count)], sum_send.at[stage])
        return jnp.sum(sums[...], axis=0)

    def dispatch(slot, start, stop):
        def go(i, _):
            z, p = peer(i)
            copy(packed.at[slot, z, p], arrived.at[slot, my_z, my_p], send_sem.at[slot], recv_sem.at[slot],
                 (z * PLANE + p, tensor))
            return 0

        lax.fori_loop(start, stop, go, 0)

    def give_back(start, stop, slot):
        def go(i, _):
            z, p = peer(i)
            copy(steps.at[slot, z, p], returned.at[slot * n_dp + me], back_send.at[slot], back_recv.at[slot],
                 (z * PLANE + p, tensor))
            return 0

        lax.fori_loop(start, stop, go, 0)

    for i in range(1, depth):
        copy(mine_z, sums_z.at[my_z], sum_send.at[0], sum_recv.at[0], (along_z(i) * PLANE + my_p, tensor))
    if bundled:
        for i in range(1, depth):
            z = along_z(i)
            copy(z_out.at[pl.ds(z * BUNDLE, BUNDLE)], z_in.at[pl.ds(my_z * BUNDLE, BUNDLE)], hop_send.at[0], hop_recv.at[0],
                 (z * PLANE + my_p, tensor))
        pltpu.make_async_copy(
            z_out.at[pl.ds(my_z * BUNDLE, BUNDLE)], z_in.at[pl.ds(my_z * BUNDLE, BUNDLE)], hop_recv.at[0]).start()
    pltpu.make_async_copy(packed.at[0, my_z, my_p], arrived.at[0, my_z, my_p], recv_sem.at[0]).start()
    dispatch(0, 1, n_dp // 2)
    tile = heard(sums_z, 0, depth - 1)
    mine_p[...] = tile
    sums_p[my_p] = tile
    for i in range(1, PLANE):
        copy(mine_p, sums_p.at[my_p], sum_send.at[1], sum_recv.at[1], (my_z * PLANE + in_plane(i), tensor))
    if bundled:
        wait(z_in, hop_recv.at[0])

        def spread(p, _):
            rank = rows_s[RANK, my_z * PLANE + p]
            for z in range(depth):
                packed[1, z, p] = z_in[z * BUNDLE + rank]
            return 0

        lax.fori_loop(0, PLANE, spread, 0)
        for i in range(1, PLANE):
            p = in_plane(i)
            copy(packed.at[1, pl.ds(0, depth), p], arrived.at[1, pl.ds(0, depth), my_p], send_sem.at[1], recv_sem.at[1],
                 (my_z * PLANE + p, tensor))
        pltpu.make_async_copy(
            packed.at[1, pl.ds(0, depth), my_p], arrived.at[1, pl.ds(0, depth), my_p], recv_sem.at[1]).start()
    else:
        dispatch(1, 1, n_dp)
        pltpu.make_async_copy(packed.at[1, my_z, my_p], arrived.at[1, my_z, my_p], recv_sem.at[1]).start()
    dispatch(0, n_dp // 2, n_dp)
    tile = heard(sums_p, 1, PLANE - 1)
    mine_y[...] = tile
    sums_y[tensor] = tile
    for i in range(1, n_tensor):
        copy(mine_y, sums_y.at[tensor], sum_send.at[2], sum_recv.at[2], (me, lax.rem(tensor + i, n_tensor)))
    tile = heard(sums_y, 2, n_tensor - 1)
    clip = lax.rsqrt(total(tile) / (blocks * n_tensor * order * order) + 1e-06)
    clip_sq = clip * clip

    eye = lax.broadcasted_iota(I32, (order, order), 0) == lax.broadcasted_iota(I32, (order, order), 1)

    def update(k, _):
        slot = slots - 1 - k
        filled = jnp.where(owned > slot, 1.0, 0.0)
        wait(arrived.at[slot], recv_sem.at[slot])
        wait(left.at[slot], state_sem.at[0, slot])
        wait(right.at[slot], state_sem.at[1, slot])
        grad = arrived[slot].reshape(order, order)
        grad_sq = total(grad * grad)
        grad = grad.astype(BF16)
        gram = clip_sq * (0.1 / order)
        left_new = 0.9 * left[slot] + gram * lax.dot_general(
            grad, grad, (((1,), (1,)), ((), ())), preferred_element_type=F32)
        left[slot] = filled * left_new
        right_new = 0.9 * right[slot] + gram * lax.dot_general(
            grad, grad, (((0,), (0,)), ((), ())), preferred_element_type=F32)
        right[slot] = filled * right_new
        pltpu.make_async_copy(left.at[slot], new_left_ref.at[slot], out_sem.at[0, slot]).start()
        pltpu.make_async_copy(right.at[slot], new_right_ref.at[slot], out_sem.at[1, slot]).start()
        left_root, left_scale = scaled_root(left_new, eye)
        right_root, right_scale = scaled_root(right_new, eye)
        middle = matmul(left_root.astype(BF16), grad).astype(BF16)
        direction = matmul(middle, right_root.astype(BF16))
        scale = clip * jnp.sqrt(jnp.sqrt(left_scale * right_scale))
        ratio = jnp.sqrt(clip_sq * grad_sq + 1e-06) * lax.rsqrt(scale * scale * total(direction * direction) + 1e-06)
        steps[slot] = ((-ratio * scale) * direction).reshape(depth, PLANE, rows, order)

        @pl.when(k == 0)
        def _():
            if bundled:
                for i in range(1, PLANE):
                    p = in_plane(i)
                    copy(steps.at[1, pl.ds(0, depth), p], x_back.at[my_p], back_send.at[1], back_recv.at[1],
                         (my_z * PLANE + p, tensor))
                pltpu.make_async_copy(steps.at[1, pl.ds(0, depth), my_p], x_back.at[my_p], back_recv.at[1]).start()
            else:
                give_back(1, n_dp, 1)
                pltpu.make_async_copy(steps.at[1, my_z, my_p], returned.at[n_dp + me], back_recv.at[1]).start()

        return 0

    lax.fori_loop(0, slots, update, 0)

    pltpu.make_async_copy(steps.at[0, my_z, my_p], returned.at[me], back_recv.at[0]).start()
    give_back(1, n_dp // 2, 0)
    if bundled:
        wait(x_back, back_recv.at[1])

        def gather(q, _):
            place = rows_s[PLACE, my_z * BUNDLE + q]
            for z in range(depth):
                z_back[z * BUNDLE + q] = x_back[place, z]
            return 0

        lax.fori_loop(0, BUNDLE, gather, 0)
        for i in range(1, depth):
            z = along_z(i)
            copy(z_back.at[pl.ds(z * BUNDLE, BUNDLE)], returned.at[pl.ds(n_dp + my_z * BUNDLE, BUNDLE)],
                 hop_send.at[1], hop_recv.at[1], (z * PLANE + my_p, tensor))
        pltpu.make_async_copy(
            z_back.at[pl.ds(my_z * BUNDLE, BUNDLE)], returned.at[pl.ds(n_dp + my_z * BUNDLE, BUNDLE)], hop_recv.at[1]).start()
    give_back(n_dp // 2, n_dp, 0)

    others = returned.at[pl.ds(0, n_dp - 1)]
    wait(others, send_sem.at[0])
    if bundled:
        wait(z_out.at[pl.ds(0, (depth - 1) * BUNDLE)], hop_send.at[0])
        wait(x_back.at[pl.ds(0, PLANE - 1)], send_sem.at[1])
        wait(x_back.at[pl.ds(0, PLANE - 1)], back_send.at[1])
    else:
        wait(others, send_sem.at[1])
        wait(others, back_send.at[1])
    for slot in range(slots):
        pltpu.make_async_copy(left.at[slot], new_left_ref.at[slot], out_sem.at[0, slot]).wait()
        pltpu.make_async_copy(right.at[slot], new_right_ref.at[slot], out_sem.at[1, slot]).wait()
    wait(others, back_send.at[0])
    if bundled:
        wait(z_out.at[pl.ds(0, (depth - 1) * BUNDLE)], hop_send.at[1])
        wait(returned.at[pl.ds(n_dp, depth * BUNDLE)], hop_recv.at[1])
    else:
        wait(returned.at[pl.ds(n_dp, n_dp)], back_recv.at[1])
    wait(returned.at[pl.ds(0, n_dp)], back_recv.at[0])

    def pick(j, _):
        step_ref[j] = returned[rows_s[PICK, j]]
        return 0

    lax.fori_loop(0, blocks, pick, 0)


def owner_step(n_dp, n_tensor, bundled, owner_map, grads, left_old, right_old):
    blocks, rows, order = grads.shape
    slots = left_old.shape[0]
    depth = n_dp // PLANE
    vmem = pl.BlockSpec(memory_space=pltpu.VMEM)
    hbm = pl.BlockSpec(memory_space=pl.ANY)
    tile = pltpu.VMEM((8, 128), F32)
    state = pltpu.VMEM((slots, order, order), F32)
    parts = pltpu.VMEM((slots, depth, PLANE, rows, order), F32)
    bundles = pltpu.VMEM((depth * BUNDLE, rows, order), F32)
    dma = pltpu.SemaphoreType.DMA
    return pl.pallas_call(
        functools.partial(kernel, n_dp, n_tensor, bundled),
        out_shape=(
            jax.ShapeDtypeStruct((blocks, rows, order), F32),
            jax.ShapeDtypeStruct((slots, order, order), F32),
            jax.ShapeDtypeStruct((slots, order, order), F32),
        ),
        in_specs=[vmem, hbm, hbm, hbm],
        out_specs=(vmem, hbm, hbm),
        scratch_shapes=[
            pltpu.VMEM((blocks, rows, order), F32),
            parts, parts, state, state, parts,
            pltpu.VMEM((slots * n_dp, rows, order), F32),
            bundles, bundles,
            pltpu.VMEM((PLANE, depth, rows, order), F32),
            bundles,
            pltpu.VMEM((depth, 8, 128), F32),
            pltpu.VMEM((PLANE, 8, 128), F32),
            pltpu.VMEM((n_tensor, 8, 128), F32),
            tile, tile, tile,
            pltpu.VMEM((8, 128), I32),
            pltpu.SMEM((8, 128), I32),
            dma((2,)), dma((2, slots)), dma((2, slots)),
            dma((slots,)), dma((slots,)), dma((slots,)), dma((slots,)),
            dma((2,)), dma((2,)), dma((3,)), dma((3,)),
        ],
        compiler_params=pltpu.CompilerParams(
            collective_id=0 if bundled else 1, has_side_effects=True, vmem_limit_bytes=48 * 2**20
        ),
        cost_estimate=pl.CostEstimate(
            flops=slots * 24 * order**3, bytes_accessed=18 * order * order, transcendentals=0),
    )(owner_map, grads, left_old, right_old)


def local(grad_blocks, owner_map, left_state, right_state):
    n_dp = lax.axis_size("dp")
    n_tensor = lax.axis_size("tensor")
    blocks = owner_map.shape[1]
    positions = jnp.arange(blocks)
    twice = (owner_map[:, :, None] == owner_map[:, None, :]) & (positions[:, None] < positions[None, :])
    at = owner_map[:, None, :, None] // PLANE == jnp.arange(n_dp // PLANE)[None, None, None, :]
    seconds = jnp.sum(jnp.where(twice[:, :, :, None] & at, 1, 0), axis=(1, 2))
    step_blocks, new_left, new_right = lax.cond(
        jnp.max(seconds) <= BUNDLE,
        functools.partial(owner_step, n_dp, n_tensor, True),
        functools.partial(owner_step, n_dp, n_tensor, False),
        owner_map, grad_blocks, left_state[0, 0], right_state[0, 0],
    )
    return (step_blocks, new_left[None, None], new_right[None, None])


def solution(mesh):
    state = P("tensor", "dp", None, None, None)
    return jax.shard_map(
        local,
        mesh=mesh,
        in_specs=(P("tensor", "dp", None), P(), state, state),
        out_specs=(P("tensor", "dp", None), state, state),
        check_vma=False,
    )
```

```python
import functools

import jax
import jax.numpy as jnp
from jax import lax
from jax.experimental import pallas as pl
from jax.experimental.pallas import tpu as pltpu
from jax.sharding import PartitionSpec as P

MESH = pl.DeviceIdType.MESH
F32 = jnp.float32
BF16 = jnp.bfloat16
I32 = jnp.int32
PLANE = 8
ROOMS = ((9, 3, 7), (12, 4, 8), (16, 8, 8))


def matmul(a, b):
    return jnp.dot(a, b, preferred_element_type=F32)


def total(x):
    return jnp.sum(x, keepdims=True)


def scaled_root(factor, eye):
    scaling = 2.5 * lax.rsqrt(total(factor * factor) + 1e-06)
    matrix = scaling * factor
    step_one = jnp.where(eye, 1.25, 0.0) - 0.25 * matrix
    step_one = step_one.astype(BF16)
    square = matmul(step_one, step_one).astype(BF16)
    fourth = matmul(square, square).astype(BF16)
    matrix = matmul(fourth, matrix.astype(BF16))
    step_two = (jnp.where(eye, 1.25, 0.0) - 0.25 * matrix).astype(BF16)
    return matmul(step_one, step_two), scaling


def square_iotas(n):
    return lax.broadcasted_iota(I32, (n, n), 0), lax.broadcasted_iota(I32, (n, n), 1)


def slots_of(owners):
    blocks = owners.shape[1]
    sub, lane = square_iotas(blocks)
    across = jnp.broadcast_to(owners, (blocks, blocks))
    owner = jnp.sum(jnp.where(sub == lane, across, 0), axis=1, keepdims=True)
    same = across == owner
    slot = jnp.sum(jnp.where(same & (lane < sub), 1, 0), axis=1, keepdims=True)
    slot_row = jnp.sum(jnp.where(same & (sub < lane), 1, 0), axis=0, keepdims=True)
    return owner, slot, slot_row, across


def gauge(owner_ref, level_ref):
    blocks = owner_ref.shape[1]
    wide = lax.broadcasted_iota(I32, (blocks, 128), 1)
    most = jnp.zeros((1, 128), I32)
    seconds = jnp.zeros((1, 128), I32)
    firsts = jnp.zeros((1, 128), I32)
    for t in range(owner_ref.shape[0]):
        owner, slot, _, _ = slots_of(owner_ref[t:t + 1, :])
        here = owner // PLANE == wide
        most = jnp.maximum(most, jnp.sum(jnp.where(here, 1, 0), axis=0, keepdims=True))
        seconds = jnp.maximum(seconds, jnp.sum(jnp.where(here & (slot == 1), 1, 0), axis=0, keepdims=True))
        firsts = jnp.maximum(firsts, jnp.sum(jnp.where(here & (slot == 0), 1, 0), axis=0, keepdims=True))
    level = jnp.zeros((1, 128), I32)
    for k, (room, early, late) in enumerate(ROOMS[:-1]):
        level = jnp.maximum(level, jnp.where((most > room) | (seconds > early) | (firsts > late), k + 1, 0))
    level_ref[0] = jnp.max(level)


BUNDLED, RANK, EARLY, LATE, PICK = range(5)


def plan(owners, me, n_dp, room, early, late):
    blocks = owners.shape[1]
    owner, slot, slot_row, across = slots_of(owners)
    z, z_row = owner // PLANE, across // PLANE
    slot_row = jnp.broadcast_to(slot_row, (blocks, blocks))
    ahead = jnp.where((z_row == z) & (slot_row == slot) & (across < owner), 1, 0)
    ahead = jnp.sum(ahead, axis=1, keepdims=True)
    rank = ahead + jnp.sum(jnp.where((z_row == z) & (slot_row > slot), 1, 0), axis=1, keepdims=True)
    wide = lax.broadcasted_iota(I32, (blocks, 128), 1)
    block = lax.broadcasted_iota(I32, (blocks, 128), 0)

    def row(where, value):
        return jnp.sum(jnp.where(where == wide, value, 0), axis=0, keepdims=True)

    place = owner % PLANE
    rows = (
        row(z * room + rank, block),
        row(slot * n_dp + owner, jnp.minimum(rank, jnp.where(slot == 1, early, room) - 1)),
        row(jnp.where(slot == 1, z * early + ahead, -1), place),
        row(jnp.where(slot == 0, z * late + ahead, -1), place),
        row(block, z * (early + late) + jnp.where(slot == 1, ahead, early + ahead)),
    )
    owned = jnp.sum(jnp.where(owners == me, 1, 0), keepdims=True)
    return jnp.concatenate(rows + rows[:3], axis=0), owned


def kernel(n_dp, n_tensor, room, early, late, depth, *refs):
    (owner_ref, grad_ref, left_ref, right_ref, step_ref, new_left_ref, new_right_ref,
     grads, packed, arrived, left, right, steps, returned, z_out, z_back,
     sums_z, sums_p, sums_y, mine_z, mine_p, mine_y, rows_v, rows_s,
     local_sem, state_sem, out_sem, z_send, z_recv, spread_send, spread_recv,
     part_send, part_recv, back_send, back_recv, sum_send, sum_recv) = refs[:-4 * depth]
    lists = refs[-4 * depth:]
    z_first, z_rest, x_second, x_first = (lists[k * depth:(k + 1) * depth] for k in range(4))
    me = lax.axis_index("dp")
    tensor = lax.axis_index("tensor")
    blocks, rows, order = grads.shape
    slots = arrived.shape[0]
    my_z = me // PLANE
    my_p = lax.rem(me, PLANE)
    offsets = [(k + 1) // 2 if k % 2 else (depth - k // 2) % depth for k in range(depth)]

    get_grads = pltpu.make_async_copy(grad_ref, grads, local_sem.at[0])
    get_grads.start()

    barrier = pltpu.get_barrier_semaphore()

    def greet(i, _):
        pl.semaphore_signal(barrier, inc=1, device_id=(my_z * PLANE + lax.rem(my_p + i, PLANE), tensor), device_id_type=MESH)
        return 0

    def greet_z(i, _):
        pl.semaphore_signal(barrier, inc=1, device_id=(lax.rem(my_z + i, depth) * PLANE + my_p, tensor), device_id_type=MESH)
        return 0

    lax.fori_loop(1, PLANE, greet, 0)
    lax.fori_loop(1, depth, greet_z, 0)
    for i in range(1, n_tensor):
        pl.semaphore_signal(barrier, inc=1, device_id=(me, lax.rem(tensor + i, n_tensor)), device_id_type=MESH)

    table, owned = plan(owner_ref[pl.ds(tensor, 1), :], me, n_dp, room, early, late)
    rows_v[...] = table
    put_rows = pltpu.make_async_copy(rows_v, rows_s, local_sem.at[1])
    put_rows.start()
    for slot in range(slots):
        pltpu.make_async_copy(left_ref.at[slot], left.at[slot], state_sem.at[0, slot]).start()
        pltpu.make_async_copy(right_ref.at[slot], right.at[slot], state_sem.at[1, slot]).start()

    get_grads.wait()
    tile = jnp.zeros((8, 128), F32)
    for k in range(order // 128):
        part = grads[:, :, k * 128:(k + 1) * 128]
        tile = tile + jnp.sum(part * part, axis=0)
    mine_z[...] = tile
    sums_z[my_z] = tile
    put_rows.wait()

    def pack(z, _):
        for q in range(room):
            z_out[z, q] = grads[rows_s[BUNDLED, z * room + q]]
        return 0

    lax.fori_loop(0, depth, pack, 0)
    z_first[0][...] = z_out[my_z, :early]
    z_rest[0][...] = z_out[my_z, early:]
    pl.semaphore_wait(barrier, PLANE + depth + n_tensor - 3)

    def copy(src, dst, send, recv, to):
        pltpu.make_async_remote_copy(
            src_ref=src, dst_ref=dst, send_sem=send, recv_sem=recv, device_id=to, device_id_type=MESH
        ).start()

    def wait(ref, sem):
        pltpu.make_async_copy(ref, ref, sem).wait()

    def along_z(i):
        return lax.rem(my_z + i, depth)

    def column(z):
        return (z * PLANE + my_p, tensor)

    def plane(i):
        p = lax.rem(my_p + i, PLANE)
        return p, (my_z * PLANE + p, tensor)

    def heard(sums, stage, count):
        wait(sums.at[pl.ds(0, count)], sum_recv.at[stage])
        wait(sums.at[pl.ds(0, count)], sum_send.at[stage])
        return jnp.sum(sums[...], axis=0)

    for i in offsets[1:]:
        z = along_z(i)
        copy(mine_z, sums_z.at[my_z], sum_send.at[0], sum_recv.at[0], column(z))
        copy(z_out.at[z, pl.ds(0, early)], z_first[i], z_send.at[1, i], z_recv.at[1, i], column(z))
    for i in offsets[1:]:
        z = along_z(i)
        copy(z_out.at[z, pl.ds(early, room - early)], z_rest[i], z_send.at[0, i], z_recv.at[0, i], column(z))

    def spread(slot, i):
        z = lax.rem(my_z + depth - i, depth)
        if i:
            wait(z_first[i] if slot else z_rest[i], z_recv.at[slot, i])

        def one(p, _):
            rank = rows_s[RANK, slot * n_dp + my_z * PLANE + p]
            if slot:
                packed[slot, p, z] = z_first[i][rank]
            else:
                before = z_first[i][jnp.minimum(rank, early - 1)]
                after = z_rest[i][jnp.maximum(rank - early, 0)]
                packed[slot, p, z] = jnp.where(rank < early, before, after)
            return 0

        lax.fori_loop(0, PLANE, one, 0)
        for k in range(1, PLANE):
            p, to = plane(k)
            copy(packed.at[slot, p, z], arrived.at[slot, z, my_p], spread_send.at[slot], spread_recv.at[slot], to)
        arrived[slot, z, my_p] = packed[slot, my_p, z]

    for i in offsets:
        spread(1, i)
    tile = heard(sums_z, 0, depth - 1)
    mine_p[...] = tile
    sums_p[my_p] = tile
    for i in range(1, PLANE):
        copy(mine_p, sums_p.at[my_p], sum_send.at[1], sum_recv.at[1], plane(i)[1])
    for i in offsets[:3]:
        spread(0, i)
    tile = heard(sums_p, 1, PLANE - 1)
    mine_y[...] = tile
    sums_y[tensor] = tile
    for i in range(1, n_tensor):
        copy(mine_y, sums_y.at[tensor], sum_send.at[2], sum_recv.at[2], (me, lax.rem(tensor + i, n_tensor)))
    for i in offsets[3:5]:
        spread(0, i)
    tile = heard(sums_y, 2, n_tensor - 1)
    clip = lax.rsqrt(total(tile) / (blocks * n_tensor * order * order) + 1e-06)
    clip_sq = clip * clip
    sub, lane = square_iotas(order)
    eye = sub == lane

    def update(slot):
        filled = jnp.where(owned > slot, 1.0, 0.0)
        wait(packed.at[slot, pl.ds(0, PLANE - 1)], spread_recv.at[slot])
        wait(left.at[slot], state_sem.at[0, slot])
        wait(right.at[slot], state_sem.at[1, slot])
        grad = arrived[slot].reshape(order, order)
        grad_sq = total(grad * grad)
        grad = grad.astype(BF16)
        gram = clip_sq * (0.1 / order)
        left_new = 0.9 * left[slot] + gram * lax.dot_general(
            grad, grad, (((1,), (1,)), ((), ())), preferred_element_type=F32)
        left[slot] = filled * left_new
        right_new = 0.9 * right[slot] + gram * lax.dot_general(
            grad, grad, (((0,), (0,)), ((), ())), preferred_element_type=F32)
        right[slot] = filled * right_new
        pltpu.make_async_copy(left.at[slot], new_left_ref.at[slot], out_sem.at[0, slot]).start()
        pltpu.make_async_copy(right.at[slot], new_right_ref.at[slot], out_sem.at[1, slot]).start()
        left_root, left_scale = scaled_root(left_new, eye)
        right_root, right_scale = scaled_root(right_new, eye)
        middle = matmul(left_root.astype(BF16), grad).astype(BF16)
        direction = matmul(middle, right_root.astype(BF16))
        scale = clip * jnp.sqrt(jnp.sqrt(left_scale * right_scale))
        ratio = jnp.sqrt(clip_sq * grad_sq + 1e-06) * lax.rsqrt(scale * scale * total(direction * direction) + 1e-06)
        steps[slot] = ((-ratio * scale) * direction).reshape(depth, PLANE, rows, order)

    def collect(slot):
        part = x_second if slot else x_first
        for i in offsets[::-1]:
            z = along_z(i)
            for k in range(1, PLANE):
                p, to = plane(k)
                copy(steps.at[slot, z, p], part[i].at[my_p], part_send.at[slot, i], part_recv.at[slot, i], to)
            part[i][my_p] = steps[slot, z, my_p]

    def send_back(slot, i):
        part = (x_second if slot else x_first)[i]
        start, size = (0, early) if slot else (early, late)
        z = along_z(i)
        wait(part.at[pl.ds(0, PLANE - 1)], part_recv.at[slot, i])

        def gather(q, _):
            z_back[z, start + q] = part[rows_s[EARLY if slot else LATE, my_z * size + q]]
            return 0

        lax.fori_loop(0, size, gather, 0)
        if i:
            copy(z_back.at[z, pl.ds(start, size)], returned.at[my_z, pl.ds(start, size)],
                 back_send.at[slot], back_recv.at[slot], column(z))

    update(1)
    for i in offsets[5:]:
        spread(0, i)
    collect(1)
    update(0)
    collect(0)
    for slot in (1, 0):
        for i in offsets[::-1]:
            send_back(slot, i)
    returned[my_z] = z_back[my_z]

    for slot in range(slots):
        pltpu.make_async_copy(left.at[slot], new_left_ref.at[slot], out_sem.at[0, slot]).wait()
        pltpu.make_async_copy(right.at[slot], new_right_ref.at[slot], out_sem.at[1, slot]).wait()
        wait(packed.at[slot, pl.ds(0, PLANE - 1)], spread_send.at[slot])
        for i in range(1, depth):
            wait(z_first[i] if slot else z_rest[i], z_send.at[slot, i])
        for i in range(depth):
            wait(x_first[i].at[pl.ds(0, PLANE - 1)], part_send.at[slot, i])
    for slot, size in ((1, early), (0, late)):
        seven = z_back.at[pl.ds(0, depth - 1), pl.ds(0, size)]
        wait(seven, back_send.at[slot])
        wait(seven, back_recv.at[slot])

    def pick(j, _):
        key = rows_s[PICK, j]
        step_ref[j] = returned[key // (early + late), lax.rem(key, early + late)]
        return 0

    lax.fori_loop(0, blocks, pick, 0)


def owner_step(n_dp, n_tensor, level, owner_map, grads, left_old, right_old):
    room, early, late = ROOMS[level]
    blocks, rows, order = grads.shape
    slots = left_old.shape[0]
    depth = n_dp // PLANE
    vmem = pl.BlockSpec(memory_space=pltpu.VMEM)
    hbm = pl.BlockSpec(memory_space=pl.ANY)
    dma = pltpu.SemaphoreType.DMA

    def pieces(*lead):
        return pltpu.VMEM(lead + (rows, order), F32)

    def tiles(*lead):
        return pltpu.VMEM(lead + (8, 128), F32)

    state = pltpu.VMEM((slots, order, order), F32)
    return pl.pallas_call(
        functools.partial(kernel, n_dp, n_tensor, room, early, late, depth),
        out_shape=(
            jax.ShapeDtypeStruct((blocks, rows, order), F32),
            jax.ShapeDtypeStruct((slots, order, order), F32),
            jax.ShapeDtypeStruct((slots, order, order), F32),
        ),
        in_specs=[vmem, hbm, hbm, hbm],
        out_specs=(vmem, hbm, hbm),
        scratch_shapes=[
            pieces(blocks), pieces(slots, PLANE, depth), pieces(slots, depth, PLANE), state, state,
            pieces(slots, depth, PLANE), pieces(depth, early + late), pieces(depth, room), pieces(depth, early + late),
            tiles(depth), tiles(PLANE), tiles(n_tensor), tiles(), tiles(), tiles(),
            pltpu.VMEM((8, 128), I32), pltpu.SMEM((8, 128), I32),
            dma((2,)), dma((2, slots)), dma((2, slots)), dma((slots, depth)), dma((slots, depth)),
            dma((slots,)), dma((slots,)), dma((slots, depth)), dma((slots, depth)), dma((slots,)), dma((slots,)),
            dma((3,)), dma((3,)),
        ] + [pieces(early)] * depth + [pieces(room - early)] * depth + [pieces(PLANE)] * (2 * depth),
        compiler_params=pltpu.CompilerParams(
            collective_id=level, has_side_effects=True, vmem_limit_bytes=48 * 2**20
        ),
        cost_estimate=pl.CostEstimate(
            flops=slots * 24 * order**3, bytes_accessed=18 * order * order, transcendentals=0),
    )(owner_map, grads, left_old, right_old)


def local(grad_blocks, owner_map, left_state, right_state):
    n_dp = lax.axis_size("dp")
    n_tensor = lax.axis_size("tensor")
    level = pl.pallas_call(
        gauge,
        out_shape=jax.ShapeDtypeStruct((1,), I32),
        in_specs=[pl.BlockSpec(memory_space=pltpu.VMEM)],
        out_specs=pl.BlockSpec(memory_space=pltpu.SMEM),
    )(owner_map)
    step_blocks, new_left, new_right = lax.switch(
        level[0],
        [functools.partial(owner_step, n_dp, n_tensor, k) for k in range(len(ROOMS))],
        owner_map, grad_blocks, left_state[0, 0], right_state[0, 0],
    )
    return (step_blocks, new_left[None, None], new_right[None, None])


def solution(mesh):
    state = P("tensor", "dp", None, None, None)
    return jax.shard_map(
        local,
        mesh=mesh,
        in_specs=(P("tensor", "dp", None), P(), state, state),
        out_specs=(P("tensor", "dp", None), state, state),
        check_vma=False,
    )
```

```python
import functools

import jax
import jax.numpy as jnp
from jax import lax
from jax.experimental import pallas as pl
from jax.experimental.pallas import tpu as pltpu
from jax.sharding import PartitionSpec as P

MESH = pl.DeviceIdType.MESH
F32 = jnp.float32
BF16 = jnp.bfloat16
I32 = jnp.int32
PLANE = 8
ROOMS = ((8, 3, 6), (9, 3, 7), (12, 4, 8), (16, 8, 8))


def matmul(a, b):
    return jnp.dot(a, b, preferred_element_type=F32)


def total(x):
    return jnp.sum(x, keepdims=True)


def scaled_root(factor, eye):
    scaling = 2.5 * lax.rsqrt(total(factor * factor) + 1e-06)
    matrix = scaling * factor
    step_one = jnp.where(eye, 1.25, 0.0) - 0.25 * matrix
    step_one = step_one.astype(BF16)
    square = matmul(step_one, step_one).astype(BF16)
    fourth = matmul(square, square).astype(BF16)
    matrix = matmul(fourth, matrix.astype(BF16))
    step_two = (jnp.where(eye, 1.25, 0.0) - 0.25 * matrix).astype(BF16)
    return matmul(step_one, step_two), scaling


def square_iotas(n):
    return lax.broadcasted_iota(I32, (n, n), 0), lax.broadcasted_iota(I32, (n, n), 1)


def slots_of(owners):
    blocks = owners.shape[1]
    sub, lane = square_iotas(blocks)
    across = jnp.broadcast_to(owners, (blocks, blocks))
    owner = jnp.sum(jnp.where(sub == lane, across, 0), axis=1, keepdims=True)
    same = across == owner
    slot = jnp.sum(jnp.where(same & (lane < sub), 1, 0), axis=1, keepdims=True)
    slot_row = jnp.sum(jnp.where(same & (sub < lane), 1, 0), axis=0, keepdims=True)
    return owner, slot, slot_row, across


def gauge(owner_ref, level_ref):
    blocks = owner_ref.shape[1]
    wide = lax.broadcasted_iota(I32, (blocks, 128), 1)
    most = jnp.zeros((1, 128), I32)
    seconds = jnp.zeros((1, 128), I32)
    firsts = jnp.zeros((1, 128), I32)
    for t in range(owner_ref.shape[0]):
        owner, slot, _, _ = slots_of(owner_ref[t:t + 1, :])
        here = owner // PLANE == wide
        most = jnp.maximum(most, jnp.sum(jnp.where(here, 1, 0), axis=0, keepdims=True))
        seconds = jnp.maximum(seconds, jnp.sum(jnp.where(here & (slot == 1), 1, 0), axis=0, keepdims=True))
        firsts = jnp.maximum(firsts, jnp.sum(jnp.where(here & (slot == 0), 1, 0), axis=0, keepdims=True))
    level = jnp.zeros((1, 128), I32)
    for k, (room, early, late) in enumerate(ROOMS[:-1]):
        level = jnp.maximum(level, jnp.where((most > room) | (seconds > early) | (firsts > late), k + 1, 0))
    level_ref[0] = jnp.max(level)


BUNDLED, RANK, EARLY, LATE, PICK = range(5)


def plan(owners, me, n_dp, room, early, late):
    blocks = owners.shape[1]
    owner, slot, slot_row, across = slots_of(owners)
    z, z_row = owner // PLANE, across // PLANE
    slot_row = jnp.broadcast_to(slot_row, (blocks, blocks))
    ahead = jnp.where((z_row == z) & (slot_row == slot) & (across < owner), 1, 0)
    ahead = jnp.sum(ahead, axis=1, keepdims=True)
    rank = ahead + jnp.sum(jnp.where((z_row == z) & (slot_row > slot), 1, 0), axis=1, keepdims=True)
    wide = lax.broadcasted_iota(I32, (blocks, 128), 1)
    block = lax.broadcasted_iota(I32, (blocks, 128), 0)

    def row(where, value):
        return jnp.sum(jnp.where(where == wide, value, 0), axis=0, keepdims=True)

    place = owner % PLANE
    rows = (
        row(z * room + rank, block),
        row(slot * n_dp + owner, jnp.minimum(rank, jnp.where(slot == 1, early, room) - 1)),
        row(jnp.where(slot == 1, z * early + ahead, -1), place),
        row(jnp.where(slot == 0, z * late + ahead, -1), place),
        row(block, z * (early + late) + jnp.where(slot == 1, ahead, early + ahead)),
    )
    owned = jnp.sum(jnp.where(owners == me, 1, 0), keepdims=True)
    return jnp.concatenate(rows + rows[:3], axis=0), owned


def kernel(n_dp, n_tensor, room, early, late, depth, *refs):
    (owner_ref, grad_ref, left_ref, right_ref, step_ref, new_left_ref, new_right_ref,
     grads, packed, arrived, left, right, steps, returned, z_out, z_back,
     sums_z, sums_p, sums_y, mine_z, mine_p, mine_y, rows_v, rows_s,
     local_sem, state_sem, out_sem, z_send, z_recv, spread_send, spread_recv,
     part_send, part_recv, back_send, back_recv, sum_send, sum_recv) = refs[:-4 * depth]
    lists = refs[-4 * depth:]
    z_first, z_rest, x_second, x_first = (lists[k * depth:(k + 1) * depth] for k in range(4))
    me = lax.axis_index("dp")
    tensor = lax.axis_index("tensor")
    blocks, rows, order = grads.shape
    slots = arrived.shape[0]
    my_z = me // PLANE
    my_p = lax.rem(me, PLANE)
    offsets = [(k + 1) // 2 if k % 2 else (depth - k // 2) % depth for k in range(depth)]

    get_grads = pltpu.make_async_copy(grad_ref, grads, local_sem.at[0])
    get_grads.start()

    barrier = pltpu.get_barrier_semaphore()

    def greet(i, _):
        pl.semaphore_signal(barrier, inc=1, device_id=(my_z * PLANE + lax.rem(my_p + i, PLANE), tensor), device_id_type=MESH)
        return 0

    def greet_z(i, _):
        pl.semaphore_signal(barrier, inc=1, device_id=(lax.rem(my_z + i, depth) * PLANE + my_p, tensor), device_id_type=MESH)
        return 0

    lax.fori_loop(1, PLANE, greet, 0)
    lax.fori_loop(1, depth, greet_z, 0)
    for i in range(1, n_tensor):
        pl.semaphore_signal(barrier, inc=1, device_id=(me, lax.rem(tensor + i, n_tensor)), device_id_type=MESH)

    table, owned = plan(owner_ref[pl.ds(tensor, 1), :], me, n_dp, room, early, late)
    rows_v[...] = table
    put_rows = pltpu.make_async_copy(rows_v, rows_s, local_sem.at[1])
    put_rows.start()
    for slot in range(slots):
        pltpu.make_async_copy(left_ref.at[slot], left.at[slot], state_sem.at[0, slot]).start()
        pltpu.make_async_copy(right_ref.at[slot], right.at[slot], state_sem.at[1, slot]).start()

    get_grads.wait()
    tile = jnp.zeros((8, 128), F32)
    for k in range(order // 128):
        part = grads[:, :, k * 128:(k + 1) * 128]
        tile = tile + jnp.sum(part * part, axis=0)
    mine_z[...] = tile
    sums_z[my_z] = tile
    put_rows.wait()

    def pack(start, stop):
        def one(z, _):
            for q in range(start, stop):
                z_out[z, q] = grads[rows_s[BUNDLED, z * room + q]]
            return 0

        lax.fori_loop(0, depth, one, 0)

    pack(0, early)
    z_first[0][...] = z_out[my_z, :early]
    pl.semaphore_wait(barrier, PLANE + depth + n_tensor - 3)

    def copy(src, dst, send, recv, to):
        pltpu.make_async_remote_copy(
            src_ref=src, dst_ref=dst, send_sem=send, recv_sem=recv, device_id=to, device_id_type=MESH
        ).start()

    def wait(ref, sem):
        pltpu.make_async_copy(ref, ref, sem).wait()

    def along_z(i):
        return lax.rem(my_z + i, depth)

    def column(z):
        return (z * PLANE + my_p, tensor)

    def plane(i):
        p = lax.rem(my_p + i, PLANE)
        return p, (my_z * PLANE + p, tensor)

    def heard(sums, stage, count):
        wait(sums.at[pl.ds(0, count)], sum_recv.at[stage])
        wait(sums.at[pl.ds(0, count)], sum_send.at[stage])
        return jnp.sum(sums[...], axis=0)

    for i in offsets[1:]:
        copy(mine_z, sums_z.at[my_z], sum_send.at[0], sum_recv.at[0], column(along_z(i)))
    for i in offsets[1:]:
        z = along_z(i)
        copy(z_out.at[z, pl.ds(0, early)], z_first[i], z_send.at[1, i], z_recv.at[1, i], column(z))
    pack(early, room)
    z_rest[0][...] = z_out[my_z, early:]
    for i in offsets[1:]:
        z = along_z(i)
        copy(z_out.at[z, pl.ds(early, room - early)], z_rest[i], z_send.at[0, i], z_recv.at[0, i], column(z))

    def spread(slot, i):
        z = lax.rem(my_z + depth - i, depth)
        if i:
            wait(z_first[i] if slot else z_rest[i], z_recv.at[slot, i])

        def one(p, _):
            rank = rows_s[RANK, slot * n_dp + my_z * PLANE + p]
            if slot:
                packed[slot, p, z] = z_first[i][rank]
            else:
                before = z_first[i][jnp.minimum(rank, early - 1)]
                after = z_rest[i][jnp.maximum(rank - early, 0)]
                packed[slot, p, z] = jnp.where(rank < early, before, after)
            return 0

        lax.fori_loop(0, PLANE, one, 0)
        for k in range(1, PLANE):
            p, to = plane(k)
            copy(packed.at[slot, p, z], arrived.at[slot, z, my_p], spread_send.at[slot], spread_recv.at[slot], to)
        arrived[slot, z, my_p] = packed[slot, my_p, z]

    spread(1, 0)
    tile = heard(sums_z, 0, depth - 1)
    mine_p[...] = tile
    sums_p[my_p] = tile
    for i in range(1, PLANE):
        copy(mine_p, sums_p.at[my_p], sum_send.at[1], sum_recv.at[1], plane(i)[1])
    for i in offsets[1:]:
        spread(1, i)
    tile = heard(sums_p, 1, PLANE - 1)
    mine_y[...] = tile
    sums_y[tensor] = tile
    for i in range(1, n_tensor):
        copy(mine_y, sums_y.at[tensor], sum_send.at[2], sum_recv.at[2], (me, lax.rem(tensor + i, n_tensor)))
    for i in offsets[:3]:
        spread(0, i)
    tile = heard(sums_y, 2, n_tensor - 1)
    clip = lax.rsqrt(total(tile) / (blocks * n_tensor * order * order) + 1e-06)
    clip_sq = clip * clip
    sub, lane = square_iotas(order)
    eye = sub == lane

    def update(slot, beside=()):
        beside = list(beside)
        filled = jnp.where(owned > slot, 1.0, 0.0)
        wait(packed.at[slot, pl.ds(0, PLANE - 1)], spread_recv.at[slot])
        wait(left.at[slot], state_sem.at[0, slot])
        wait(right.at[slot], state_sem.at[1, slot])
        grad = arrived[slot].reshape(order, order)
        grad_sq = total(grad * grad)
        grad = grad.astype(BF16)
        gram = clip_sq * (0.1 / order)
        left_new = 0.9 * left[slot] + gram * lax.dot_general(
            grad, grad, (((1,), (1,)), ((), ())), preferred_element_type=F32)
        left[slot] = filled * left_new
        right_new = 0.9 * right[slot] + gram * lax.dot_general(
            grad, grad, (((0,), (0,)), ((), ())), preferred_element_type=F32)
        right[slot] = filled * right_new
        pltpu.make_async_copy(left.at[slot], new_left_ref.at[slot], out_sem.at[0, slot]).start()
        pltpu.make_async_copy(right.at[slot], new_right_ref.at[slot], out_sem.at[1, slot]).start()
        left_root, left_scale = scaled_root(left_new, eye)
        for i in beside[:2]:
            send_back(1, i)
        right_root, right_scale = scaled_root(right_new, eye)
        for i in beside[2:]:
            send_back(1, i)
        middle = matmul(left_root.astype(BF16), grad).astype(BF16)
        direction = matmul(middle, right_root.astype(BF16))
        scale = clip * jnp.sqrt(jnp.sqrt(left_scale * right_scale))
        ratio = jnp.sqrt(clip_sq * grad_sq + 1e-06) * lax.rsqrt(scale * scale * total(direction * direction) + 1e-06)
        steps[slot] = ((-ratio * scale) * direction).reshape(depth, PLANE, rows, order)

    def collect(slot, i):
        part = (x_second if slot else x_first)[i]
        z = along_z(i)
        for k in range(1, PLANE):
            p, to = plane(k)
            copy(steps.at[slot, z, p], part.at[my_p], part_send.at[slot, i], part_recv.at[slot, i], to)
        part[my_p] = steps[slot, z, my_p]

    def send_back(slot, i):
        part = (x_second if slot else x_first)[i]
        start, size = (0, early) if slot else (early, late)
        z = along_z(i)
        wait(part.at[pl.ds(0, PLANE - 1)], part_recv.at[slot, i])

        def gather(q, _):
            z_back[z, start + q] = part[rows_s[EARLY if slot else LATE, my_z * size + q]]
            return 0

        lax.fori_loop(0, size, gather, 0)
        if i:
            copy(z_back.at[z, pl.ds(start, size)], returned.at[my_z, pl.ds(start, size)],
                 back_send.at[slot], back_recv.at[slot], column(z))

    back = offsets[::-1]
    update(1)
    for i in offsets[3:]:
        spread(0, i)
    for i in back:
        collect(1, i)
    update(0, back[:4])
    for i in back[4:6]:
        send_back(1, i)
    for i in back:
        collect(0, i)
    for i in back[6:]:
        send_back(1, i)
    for i in back:
        send_back(0, i)
    returned[my_z] = z_back[my_z]

    for slot in range(slots):
        pltpu.make_async_copy(left.at[slot], new_left_ref.at[slot], out_sem.at[0, slot]).wait()
        pltpu.make_async_copy(right.at[slot], new_right_ref.at[slot], out_sem.at[1, slot]).wait()
        wait(packed.at[slot, pl.ds(0, PLANE - 1)], spread_send.at[slot])
        for i in range(1, depth):
            wait(z_first[i] if slot else z_rest[i], z_send.at[slot, i])
        for i in range(depth):
            wait(x_first[i].at[pl.ds(0, PLANE - 1)], part_send.at[slot, i])
    for slot, size in ((1, early), (0, late)):
        seven = z_back.at[pl.ds(0, depth - 1), pl.ds(0, size)]
        wait(seven, back_send.at[slot])
        wait(seven, back_recv.at[slot])

    def pick(j, _):
        key = rows_s[PICK, j]
        step_ref[j] = returned[key // (early + late), lax.rem(key, early + late)]
        return 0

    lax.fori_loop(0, blocks, pick, 0)


def owner_step(n_dp, n_tensor, level, owner_map, grads, left_old, right_old):
    room, early, late = ROOMS[level]
    blocks, rows, order = grads.shape
    slots = left_old.shape[0]
    depth = n_dp // PLANE
    vmem = pl.BlockSpec(memory_space=pltpu.VMEM)
    hbm = pl.BlockSpec(memory_space=pl.ANY)
    dma = pltpu.SemaphoreType.DMA

    def pieces(*lead):
        return pltpu.VMEM(lead + (rows, order), F32)

    def tiles(*lead):
        return pltpu.VMEM(lead + (8, 128), F32)

    state = pltpu.VMEM((slots, order, order), F32)
    return pl.pallas_call(
        functools.partial(kernel, n_dp, n_tensor, room, early, late, depth),
        out_shape=(
            jax.ShapeDtypeStruct((blocks, rows, order), F32),
            jax.ShapeDtypeStruct((slots, order, order), F32),
            jax.ShapeDtypeStruct((slots, order, order), F32),
        ),
        in_specs=[vmem, hbm, hbm, hbm],
        out_specs=(vmem, hbm, hbm),
        scratch_shapes=[
            pieces(blocks), pieces(slots, PLANE, depth), pieces(slots, depth, PLANE), state, state,
            pieces(slots, depth, PLANE), pieces(depth, early + late), pieces(depth, room), pieces(depth, early + late),
            tiles(depth), tiles(PLANE), tiles(n_tensor), tiles(), tiles(), tiles(),
            pltpu.VMEM((8, 128), I32), pltpu.SMEM((8, 128), I32),
            dma((2,)), dma((2, slots)), dma((2, slots)), dma((slots, depth)), dma((slots, depth)),
            dma((slots,)), dma((slots,)), dma((slots, depth)), dma((slots, depth)), dma((slots,)), dma((slots,)),
            dma((3,)), dma((3,)),
        ] + [pieces(early)] * depth + [pieces(room - early)] * depth + [pieces(PLANE)] * (2 * depth),
        compiler_params=pltpu.CompilerParams(
            collective_id=level, has_side_effects=True, vmem_limit_bytes=48 * 2**20
        ),
        cost_estimate=pl.CostEstimate(
            flops=slots * 24 * order**3, bytes_accessed=18 * order * order, transcendentals=0),
    )(owner_map, grads, left_old, right_old)


def local(grad_blocks, owner_map, left_state, right_state):
    n_dp = lax.axis_size("dp")
    n_tensor = lax.axis_size("tensor")
    level = pl.pallas_call(
        gauge,
        out_shape=jax.ShapeDtypeStruct((1,), I32),
        in_specs=[pl.BlockSpec(memory_space=pltpu.VMEM)],
        out_specs=pl.BlockSpec(memory_space=pltpu.SMEM),
    )(owner_map)
    step_blocks, new_left, new_right = lax.switch(
        level[0],
        [functools.partial(owner_step, n_dp, n_tensor, k) for k in range(len(ROOMS))],
        owner_map, grad_blocks, left_state[0, 0], right_state[0, 0],
    )
    return (step_blocks, new_left[None, None], new_right[None, None])


def solution(mesh):
    state = P("tensor", "dp", None, None, None)
    return jax.shard_map(
        local,
        mesh=mesh,
        in_specs=(P("tensor", "dp", None), P(), state, state),
        out_specs=(P("tensor", "dp", None), state, state),
        check_vma=False,
    )
```

```python
import functools

import jax
import jax.numpy as jnp
from jax import lax
from jax.experimental import pallas as pl
from jax.experimental.pallas import tpu as pltpu
from jax.sharding import PartitionSpec as P

MESH = pl.DeviceIdType.MESH
F32 = jnp.float32
BF16 = jnp.bfloat16
I32 = jnp.int32
PLANE = 8
ROOMS = ((9, 3, 7), (12, 4, 8), (16, 8, 8))


def matmul(a, b):
    return jnp.dot(a, b, preferred_element_type=F32)


def total(x):
    return jnp.sum(x, keepdims=True)


def scaled_root(factor, eye):
    scaling = 2.5 * lax.rsqrt(total(factor * factor) + 1e-06)
    matrix = scaling * factor
    step_one = jnp.where(eye, 1.25, 0.0) - 0.25 * matrix
    step_one = step_one.astype(BF16)
    square = matmul(step_one, step_one).astype(BF16)
    fourth = matmul(square, square).astype(BF16)
    matrix = matmul(fourth, matrix.astype(BF16))
    step_two = (jnp.where(eye, 1.25, 0.0) - 0.25 * matrix).astype(BF16)
    return matmul(step_one, step_two), scaling


def square_iotas(n):
    return lax.broadcasted_iota(I32, (n, n), 0), lax.broadcasted_iota(I32, (n, n), 1)


def slots_of(owners):
    blocks = owners.shape[1]
    sub, lane = square_iotas(blocks)
    across = jnp.broadcast_to(owners, (blocks, blocks))
    owner = jnp.sum(jnp.where(sub == lane, across, 0), axis=1, keepdims=True)
    same = across == owner
    slot = jnp.sum(jnp.where(same & (lane < sub), 1, 0), axis=1, keepdims=True)
    slot_row = jnp.sum(jnp.where(same & (sub < lane), 1, 0), axis=0, keepdims=True)
    return owner, slot, slot_row, across


def gauge(owner_ref, level_ref):
    blocks = owner_ref.shape[1]
    wide = lax.broadcasted_iota(I32, (blocks, 128), 1)
    most = jnp.zeros((1, 128), I32)
    seconds = jnp.zeros((1, 128), I32)
    firsts = jnp.zeros((1, 128), I32)
    for t in range(owner_ref.shape[0]):
        owner, slot, _, _ = slots_of(owner_ref[t:t + 1, :])
        here = owner // PLANE == wide
        most = jnp.maximum(most, jnp.sum(jnp.where(here, 1, 0), axis=0, keepdims=True))
        seconds = jnp.maximum(seconds, jnp.sum(jnp.where(here & (slot == 1), 1, 0), axis=0, keepdims=True))
        firsts = jnp.maximum(firsts, jnp.sum(jnp.where(here & (slot == 0), 1, 0), axis=0, keepdims=True))
    level = jnp.zeros((1, 128), I32)
    for k, (room, early, late) in enumerate(ROOMS[:-1]):
        level = jnp.maximum(level, jnp.where((most > room) | (seconds > early) | (firsts > late), k + 1, 0))
    level_ref[0] = jnp.max(level)


BUNDLED, RANK, EARLY, LATE, PICK = range(5)


def plan(owners, me, n_dp, room, early, late):
    blocks = owners.shape[1]
    owner, slot, slot_row, across = slots_of(owners)
    z, z_row = owner // PLANE, across // PLANE
    slot_row = jnp.broadcast_to(slot_row, (blocks, blocks))
    ahead = jnp.where((z_row == z) & (slot_row == slot) & (across < owner), 1, 0)
    ahead = jnp.sum(ahead, axis=1, keepdims=True)
    rank = ahead + jnp.sum(jnp.where((z_row == z) & (slot_row > slot), 1, 0), axis=1, keepdims=True)
    wide = lax.broadcasted_iota(I32, (blocks, 128), 1)
    block = lax.broadcasted_iota(I32, (blocks, 128), 0)

    def row(where, value):
        return jnp.sum(jnp.where(where == wide, value, 0), axis=0, keepdims=True)

    place = owner % PLANE
    rows = (
        row(z * room + rank, block),
        row(slot * n_dp + owner, jnp.minimum(rank, jnp.where(slot == 1, early, room) - 1)),
        row(jnp.where(slot == 1, z * early + ahead, -1), place),
        row(jnp.where(slot == 0, z * late + ahead, -1), place),
        row(block, z * (early + late) + jnp.where(slot == 1, ahead, early + ahead)),
    )
    owned = jnp.sum(jnp.where(owners == me, 1, 0), keepdims=True)
    return jnp.concatenate(rows + rows[:3], axis=0), owned


def kernel(n_dp, n_tensor, room, early, late, depth, *refs):
    (owner_ref, grad_ref, left_ref, right_ref, step_ref, new_left_ref, new_right_ref,
     grads, packed, arrived, left, right, steps, returned, z_out, z_back,
     sums_z, sums_p, sums_y, mine_z, mine_p, mine_y, rows_v, rows_s,
     local_sem, state_sem, out_sem, z_send, z_recv, spread_send, spread_recv,
     part_send, part_recv, back_send, back_recv, sum_send, sum_recv) = refs[:-4 * depth]
    lists = refs[-4 * depth:]
    z_first, z_rest, x_second, x_first = (lists[k * depth:(k + 1) * depth] for k in range(4))
    me = lax.axis_index("dp")
    tensor = lax.axis_index("tensor")
    blocks, rows, order = grads.shape
    slots = arrived.shape[0]
    my_z = me // PLANE
    my_p = lax.rem(me, PLANE)
    offsets = [(k + 1) // 2 if k % 2 else (depth - k // 2) % depth for k in range(depth)]

    get_grads = pltpu.make_async_copy(grad_ref, grads, local_sem.at[0])
    get_grads.start()

    barrier = pltpu.get_barrier_semaphore()

    def greet(i, _):
        pl.semaphore_signal(barrier, inc=1, device_id=(my_z * PLANE + lax.rem(my_p + i, PLANE), tensor), device_id_type=MESH)
        return 0

    def greet_z(i, _):
        pl.semaphore_signal(barrier, inc=1, device_id=(lax.rem(my_z + i, depth) * PLANE + my_p, tensor), device_id_type=MESH)
        return 0

    lax.fori_loop(1, PLANE, greet, 0)
    lax.fori_loop(1, depth, greet_z, 0)
    for i in range(1, n_tensor):
        pl.semaphore_signal(barrier, inc=1, device_id=(me, lax.rem(tensor + i, n_tensor)), device_id_type=MESH)

    table, owned = plan(owner_ref[pl.ds(tensor, 1), :], me, n_dp, room, early, late)
    rows_v[...] = table
    put_rows = pltpu.make_async_copy(rows_v, rows_s, local_sem.at[1])
    put_rows.start()
    for slot in range(slots):
        pltpu.make_async_copy(left_ref.at[slot], left.at[slot], state_sem.at[0, slot]).start()
        pltpu.make_async_copy(right_ref.at[slot], right.at[slot], state_sem.at[1, slot]).start()

    get_grads.wait()
    tile = jnp.zeros((8, 128), F32)
    for k in range(order // 128):
        part = grads[:, :, k * 128:(k + 1) * 128]
        tile = tile + jnp.sum(part * part, axis=0)
    mine_z[...] = tile
    sums_z[my_z] = tile
    put_rows.wait()

    def pack(start, stop):
        def one(z, _):
            for q in range(start, stop):
                z_out[z, q] = grads[rows_s[BUNDLED, z * room + q]]
            return 0

        lax.fori_loop(0, depth, one, 0)

    pack(0, early)
    z_first[0][...] = z_out[my_z, :early]
    pl.semaphore_wait(barrier, PLANE + depth + n_tensor - 3)

    def copy(src, dst, send, recv, to):
        pltpu.make_async_remote_copy(
            src_ref=src, dst_ref=dst, send_sem=send, recv_sem=recv, device_id=to, device_id_type=MESH
        ).start()

    def wait(ref, sem):
        pltpu.make_async_copy(ref, ref, sem).wait()

    def along_z(i):
        return lax.rem(my_z + i, depth)

    def column(z):
        return (z * PLANE + my_p, tensor)

    def plane(i):
        p = lax.rem(my_p + i, PLANE)
        return p, (my_z * PLANE + p, tensor)

    def heard(sums, stage, count):
        wait(sums.at[pl.ds(0, count)], sum_recv.at[stage])
        wait(sums.at[pl.ds(0, count)], sum_send.at[stage])
        return jnp.sum(sums[...], axis=0)

    for i in offsets[1:]:
        copy(mine_z, sums_z.at[my_z], sum_send.at[0], sum_recv.at[0], column(along_z(i)))
    for i in offsets[1:]:
        z = along_z(i)
        copy(z_out.at[z, pl.ds(0, early)], z_first[i], z_send.at[1, i], z_recv.at[1, i], column(z))
    pack(early, room)
    z_rest[0][...] = z_out[my_z, early:]
    for i in offsets[1:]:
        z = along_z(i)
        copy(z_out.at[z, pl.ds(early, room - early)], z_rest[i], z_send.at[0, i], z_recv.at[0, i], column(z))

    def spread(slot, i):
        z = lax.rem(my_z + depth - i, depth)
        if i:
            wait(z_first[i] if slot else z_rest[i], z_recv.at[slot, i])

        def one(p, _):
            rank = rows_s[RANK, slot * n_dp + my_z * PLANE + p]
            if slot:
                packed[slot, p, z] = z_first[i][rank]
            else:
                before = z_first[i][jnp.minimum(rank, early - 1)]
                after = z_rest[i][jnp.maximum(rank - early, 0)]
                packed[slot, p, z] = jnp.where(rank < early, before, after)
            return 0

        lax.fori_loop(0, PLANE, one, 0)
        for k in range(1, PLANE):
            p, to = plane(k)
            copy(packed.at[slot, p, z], arrived.at[slot, z, my_p], spread_send.at[slot], spread_recv.at[slot], to)
        arrived[slot, z, my_p] = packed[slot, my_p, z]

    spread(1, 0)
    tile = heard(sums_z, 0, depth - 1)
    mine_p[...] = tile
    sums_p[my_p] = tile
    for i in range(1, PLANE):
        copy(mine_p, sums_p.at[my_p], sum_send.at[1], sum_recv.at[1], plane(i)[1])
    for i in offsets[1:]:
        spread(1, i)
    tile = heard(sums_p, 1, PLANE - 1)
    mine_y[...] = tile
    sums_y[tensor] = tile
    for i in range(1, n_tensor):
        copy(mine_y, sums_y.at[tensor], sum_send.at[2], sum_recv.at[2], (me, lax.rem(tensor + i, n_tensor)))
    for i in offsets[:3]:
        spread(0, i)
    tile = heard(sums_y, 2, n_tensor - 1)
    clip = lax.rsqrt(total(tile) / (blocks * n_tensor * order * order) + 1e-06)
    clip_sq = clip * clip
    sub, lane = square_iotas(order)
    eye = sub == lane

    def update(slot, beside=()):
        beside = list(beside)
        filled = jnp.where(owned > slot, 1.0, 0.0)
        wait(packed.at[slot, pl.ds(0, PLANE - 1)], spread_recv.at[slot])
        wait(left.at[slot], state_sem.at[0, slot])
        wait(right.at[slot], state_sem.at[1, slot])
        grad = arrived[slot].reshape(order, order)
        grad_sq = total(grad * grad)
        grad = grad.astype(BF16)
        gram = clip_sq * (0.1 / order)
        left_new = 0.9 * left[slot] + gram * lax.dot_general(
            grad, grad, (((1,), (1,)), ((), ())), preferred_element_type=F32)
        left[slot] = filled * left_new
        right_new = 0.9 * right[slot] + gram * lax.dot_general(
            grad, grad, (((0,), (0,)), ((), ())), preferred_element_type=F32)
        right[slot] = filled * right_new
        pltpu.make_async_copy(left.at[slot], new_left_ref.at[slot], out_sem.at[0, slot]).start()
        pltpu.make_async_copy(right.at[slot], new_right_ref.at[slot], out_sem.at[1, slot]).start()
        left_root, left_scale = scaled_root(left_new, eye)
        for i in beside[:2]:
            send_back(1, i)
        right_root, right_scale = scaled_root(right_new, eye)
        for i in beside[2:]:
            send_back(1, i)
        middle = matmul(left_root.astype(BF16), grad).astype(BF16)
        direction = matmul(middle, right_root.astype(BF16))
        scale = clip * jnp.sqrt(jnp.sqrt(left_scale * right_scale))
        ratio = jnp.sqrt(clip_sq * grad_sq + 1e-06) * lax.rsqrt(scale * scale * total(direction * direction) + 1e-06)
        steps[slot] = ((-ratio * scale) * direction).reshape(depth, PLANE, rows, order)

    def collect(slot, i):
        part = (x_second if slot else x_first)[i]
        z = along_z(i)
        for k in range(1, PLANE):
            p, to = plane(k)
            copy(steps.at[slot, z, p], part.at[my_p], part_send.at[slot, i], part_recv.at[slot, i], to)
        part[my_p] = steps[slot, z, my_p]

    def send_back(slot, i):
        part = (x_second if slot else x_first)[i]
        start, size = (0, early) if slot else (early, late)
        z = along_z(i)
        wait(part.at[pl.ds(0, PLANE - 1)], part_recv.at[slot, i])

        def gather(q, _):
            z_back[z, start + q] = part[rows_s[EARLY if slot else LATE, my_z * size + q]]
            return 0

        lax.fori_loop(0, size, gather, 0)
        if i:
            copy(z_back.at[z, pl.ds(start, size)], returned.at[my_z, pl.ds(start, size)],
                 back_send.at[slot], back_recv.at[slot], column(z))

    back = offsets[::-1]
    update(1)
    for i in offsets[3:]:
        spread(0, i)
    for i in back:
        collect(1, i)
    update(0, back[:4])
    for i in back[4:6]:
        send_back(1, i)
    for i in back:
        collect(0, i)
    for i in back[6:]:
        send_back(1, i)
    for i in back:
        send_back(0, i)
    returned[my_z] = z_back[my_z]

    for slot in range(slots):
        pltpu.make_async_copy(left.at[slot], new_left_ref.at[slot], out_sem.at[0, slot]).wait()
        pltpu.make_async_copy(right.at[slot], new_right_ref.at[slot], out_sem.at[1, slot]).wait()
        wait(packed.at[slot, pl.ds(0, PLANE - 1)], spread_send.at[slot])
        for i in range(1, depth):
            wait(z_first[i] if slot else z_rest[i], z_send.at[slot, i])
        for i in range(depth):
            wait(x_first[i].at[pl.ds(0, PLANE - 1)], part_send.at[slot, i])
    for slot, size in ((1, early), (0, late)):
        seven = z_back.at[pl.ds(0, depth - 1), pl.ds(0, size)]
        wait(seven, back_send.at[slot])
        wait(seven, back_recv.at[slot])

    def pick(j, _):
        key = rows_s[PICK, j]
        step_ref[j] = returned[key // (early + late), lax.rem(key, early + late)]
        return 0

    lax.fori_loop(0, blocks, pick, 0)


def owner_step(n_dp, n_tensor, level, owner_map, grads, left_old, right_old):
    room, early, late = ROOMS[level]
    blocks, rows, order = grads.shape
    slots = left_old.shape[0]
    depth = n_dp // PLANE
    vmem = pl.BlockSpec(memory_space=pltpu.VMEM)
    hbm = pl.BlockSpec(memory_space=pl.ANY)
    dma = pltpu.SemaphoreType.DMA

    def pieces(*lead):
        return pltpu.VMEM(lead + (rows, order), F32)

    def tiles(*lead):
        return pltpu.VMEM(lead + (8, 128), F32)

    state = pltpu.VMEM((slots, order, order), F32)
    return pl.pallas_call(
        functools.partial(kernel, n_dp, n_tensor, room, early, late, depth),
        out_shape=(
            jax.ShapeDtypeStruct((blocks, rows, order), F32),
            jax.ShapeDtypeStruct((slots, order, order), F32),
            jax.ShapeDtypeStruct((slots, order, order), F32),
        ),
        in_specs=[vmem, hbm, hbm, hbm],
        out_specs=(vmem, hbm, hbm),
        scratch_shapes=[
            pieces(blocks), pieces(slots, PLANE, depth), pieces(slots, depth, PLANE), state, state,
            pieces(slots, depth, PLANE), pieces(depth, early + late), pieces(depth, room), pieces(depth, early + late),
            tiles(depth), tiles(PLANE), tiles(n_tensor), tiles(), tiles(), tiles(),
            pltpu.VMEM((8, 128), I32), pltpu.SMEM((8, 128), I32),
            dma((2,)), dma((2, slots)), dma((2, slots)), dma((slots, depth)), dma((slots, depth)),
            dma((slots,)), dma((slots,)), dma((slots, depth)), dma((slots, depth)), dma((slots,)), dma((slots,)),
            dma((3,)), dma((3,)),
        ] + [pieces(early)] * depth + [pieces(room - early)] * depth + [pieces(PLANE)] * (2 * depth),
        compiler_params=pltpu.CompilerParams(
            collective_id=level, has_side_effects=True, vmem_limit_bytes=48 * 2**20
        ),
        cost_estimate=pl.CostEstimate(
            flops=slots * 24 * order**3, bytes_accessed=18 * order * order, transcendentals=0),
    )(owner_map, grads, left_old, right_old)


def local(grad_blocks, owner_map, left_state, right_state):
    n_dp = lax.axis_size("dp")
    n_tensor = lax.axis_size("tensor")
    level = pl.pallas_call(
        gauge,
        out_shape=jax.ShapeDtypeStruct((1,), I32),
        in_specs=[pl.BlockSpec(memory_space=pltpu.VMEM)],
        out_specs=pl.BlockSpec(memory_space=pltpu.SMEM),
    )(owner_map)
    step_blocks, new_left, new_right = lax.switch(
        level[0],
        [functools.partial(owner_step, n_dp, n_tensor, k) for k in range(len(ROOMS))],
        owner_map, grad_blocks, left_state[0, 0], right_state[0, 0],
    )
    return (step_blocks, new_left[None, None], new_right[None, None])


def solution(mesh):
    state = P("tensor", "dp", None, None, None)
    return jax.shard_map(
        local,
        mesh=mesh,
        in_specs=(P("tensor", "dp", None), P(), state, state),
        out_specs=(P("tensor", "dp", None), state, state),
        check_vma=False,
    )
```
